512 devices in a mesh: gx: 32 (over z, x_hi), gy: 16 (over x_lo, y, core).
Axes of the slice: x: 4 (x_hi: 2, x_lo: 2; x = x_hi * 2 + x_lo), y: 4, z: 16, core: 2. Of those that a mesh axis runs over, the one named last changes fastest.
Arguments:
- source: bfloat16 [32, 16, 1280, 256], P('gx', 'gy'), may hold values from -6 to 6
- op_blocks: bfloat16 [32, 16, 10240, 128], P('gx', 'gy'), may hold values from -0.125 to 0.125
- op_in: int32 [32, 16, 80], P('gx', 'gy'), may hold values from 0 to 17, as said below
- op_out: int32 [32, 16, 80], P('gx', 'gy'), may hold values from 0 to 9, as said below
- op_count: int32 [32, 16], P('gx', 'gy'), may hold values from 24 to 80, as said below
- edge_up: int32 [32, 16, 2], P('gx', 'gy'), may hold values from 0 to 9, as said below
- edge_down: int32 [32, 16, 2], P('gx', 'gy'), may hold values from 0 to 9, as said below
Outputs:
- traces: bfloat16 [32, 16, 1280, 256], P('gx', 'gy')
The draws below stay inside these ranges and needn't reach their ends.
Inputs may be any that keep to these rules, and one draw needn't show every extreme that they name: `op_in`: the first 18 slots of each subdomain name every input block once. `op_out`: the first 10 slots of each subdomain name every output block once. `op_count`: a multiple of 8; in every draw some subdomain has all 80 slots live. `edge_up`: distinct within a subdomain. `edge_down`: distinct within a subdomain.
All inputs are finite; a program needn't handle non-finite values.
Results may differ from the reference program's by a relative error of at most 0.0039.
Values may be sent and summed in bfloat16 or wider, within the bound.
A program may use at most 128 MiB of HBM per device.

```python
import jax
import jax.numpy as jnp
from jax import lax

BS = 128
R = 256
FX = 2
EMAX = 2
NNZ = 80
ITERS = 4
NB = 10
NI = 18
N_GX = 32
N_GY = 16


def covering_list(key, cover, length):
    first_key, rest_key = jax.random.split(key)
    head_part = jax.random.permutation(first_key, cover).astype(jnp.int32)
    tail_part = jax.random.randint(rest_key, (length - cover,), 0, cover).astype(jnp.int32)
    return jnp.concatenate([head_part, tail_part])


def draw_op_in(key, part):
    key = jax.random.fold_in(key, 11)
    keys = jax.random.split(key, N_GX * N_GY)
    lists = jax.vmap(lambda single: covering_list(single, NI, NNZ))(keys)
    return lists.reshape(N_GX, N_GY, NNZ)


def draw_op_out(key, part):
    key = jax.random.fold_in(key, 23)
    keys = jax.random.split(key, N_GX * N_GY)
    lists = jax.vmap(lambda single: covering_list(single, NB, NNZ))(keys)
    return lists.reshape(N_GX, N_GY, NNZ)


def draw_op_count(key, part):
    key = jax.random.fold_in(key, 37)
    base_key, heavy_key, select_key, place_key = jax.random.split(key, 4)
    base_counts = 8 * jax.random.randint(base_key, (N_GX * N_GY,), 3, 7)
    heavy_counts = 8 * jax.random.randint(heavy_key, (N_GX * N_GY,), 7, NNZ // 8 + 1)
    selected = jax.random.randint(select_key, (N_GX * N_GY,), 0, 8) == 0
    counts_flat = jnp.where(selected, heavy_counts, base_counts)
    position = jax.random.randint(place_key, (), 0, N_GX * N_GY)
    counts_flat = jnp.where(jnp.arange(N_GX * N_GY) == position, NNZ, counts_flat)
    return counts_flat.astype(jnp.int32).reshape(N_GX, N_GY)


def edge_lists(key):
    keys = jax.random.split(key, N_GX * N_GY)
    lists = jax.vmap(lambda single: jax.random.permutation(single, NB)[:EMAX])(keys)
    return lists.astype(jnp.int32).reshape(N_GX, N_GY, EMAX)


def draw_edge_up(key, part):
    key = jax.random.fold_in(key, 41)
    return edge_lists(key)


def draw_edge_down(key, part):
    key = jax.random.fold_in(key, 53)
    return edge_lists(key)


def level_of(own_key, extent, cuts, smallest, largest):
    def one(dim, parts):
        heights = jax.random.uniform(jax.random.fold_in(jax.random.fold_in(own_key, 6), dim), (parts,), jnp.float32, smallest / len(cuts), largest / len(cuts))
        return jnp.repeat(jnp.exp(heights), extent[dim] // parts).reshape((-1,) + (1,) * (len(extent) - dim - 1))

    factor_of = one(*cuts[0])
    for cut in cuts[1:]:
        factor_of = factor_of * one(*cut)
    return factor_of


def scatter_about(rng, extent, spread, reach, cuts=(), kind=jnp.bfloat16):
    drawn = spread * jax.random.normal(rng, extent, jnp.float32)
    if cuts:
        drawn = drawn * level_of(rng, extent, cuts, -0.22, 0.18)
    return jnp.clip(drawn, -reach, reach).astype(kind)


def setup_inputs(seed: int = 0) -> dict:
    splits = jax.random.split(jax.random.key(seed), 8)
    return {
        "source": scatter_about(splits[0], (N_GX, N_GY, NB * BS, R), 1.0, 6.0, ((0, 32), (1, 16))),
        "op_blocks": scatter_about(splits[1], (N_GX, N_GY, NNZ * BS, BS), (2 * BS * NNZ // NB) ** -0.5, 0.125, ((0, 32), (1, 16))),
        "op_in": draw_op_in(jax.random.fold_in(splits[7], 71), 0),
        "op_out": draw_op_out(jax.random.fold_in(splits[7], 71), 0),
        "op_count": draw_op_count(jax.random.fold_in(splits[7], 71), 0),
        "edge_up": draw_edge_up(jax.random.fold_in(splits[7], 71), 0),
        "edge_down": draw_edge_down(jax.random.fold_in(splits[7], 71), 0),
    }


def gather_inputs(trace_all, edge_up, edge_down):
    from_left = jnp.roll(trace_all[:, :, NB - FX:], 1, axis=0)
    from_right = jnp.roll(trace_all[:, :, :FX], -1, axis=0)
    up_pick = jnp.take_along_axis(trace_all, edge_up[:, :, :, None, None].astype(jnp.int32), axis=2)
    down_pick = jnp.take_along_axis(trace_all, edge_down[:, :, :, None, None].astype(jnp.int32), axis=2)
    zero_row = jnp.zeros_like(up_pick[:, :1])
    from_below = jnp.concatenate([zero_row, up_pick[:, :-1]], axis=1)
    from_above = jnp.concatenate([down_pick[:, 1:], zero_row], axis=1)
    return jnp.concatenate([from_left, trace_all, from_right, from_below, from_above], axis=2)


def device_sweep(packed):
    source_blocks, inputs, block_groups, in_groups, out_groups, live_count = packed
    block_ids = jnp.arange(NB).astype(jnp.int32)

    def add_group(group_index, totals):
        blocks_now = block_groups[group_index].astype(jnp.float32)
        picked = inputs[in_groups[group_index]].astype(jnp.float32)
        products = jnp.einsum("ekm,emr->ekr", blocks_now, picked, precision=lax.Precision.HIGHEST)
        onehot = (out_groups[group_index][:, None] == block_ids[None, :]).astype(jnp.float32)
        return totals + jnp.einsum("eb,ekr->bkr", onehot, products, precision=lax.Precision.HIGHEST)

    totals = lax.fori_loop(0, live_count // 8, add_group, jnp.zeros((NB, BS, R), jnp.float32))
    return (source_blocks.astype(jnp.float32) + totals).astype(jnp.bfloat16)


def reference(source, op_blocks, op_in, op_out, op_count, edge_up, edge_down):
    grid_x = source.shape[0]
    grid_y = source.shape[1]
    devices_all = grid_x * grid_y
    source_blocks = source.reshape(grid_x, grid_y, NB, BS, R)
    block_groups = op_blocks.reshape(devices_all, NNZ // 8, 8, BS, BS)
    in_groups = op_in.reshape(devices_all, NNZ // 8, 8)
    out_groups = op_out.reshape(devices_all, NNZ // 8, 8)
    counts_flat = op_count.reshape(devices_all)
    source_flat = source_blocks.reshape(devices_all, NB, BS, R)
    trace_all = source_blocks
    for sweep_index in range(ITERS):
        inputs = gather_inputs(trace_all, edge_up, edge_down).reshape(devices_all, NI, BS, R)
        updated = lax.map(device_sweep, (source_flat, inputs, block_groups, in_groups, out_groups, counts_flat))
        trace_all = updated.reshape(grid_x, grid_y, NB, BS, R)
    return trace_all.reshape(grid_x, grid_y, NB * BS, R)
```

```python
import functools

import jax
import jax.numpy as jnp
from jax import lax
from jax.experimental import pallas as pl
from jax.experimental.pallas import tpu as pltpu
from jax.sharding import PartitionSpec as P

FX = 2
EMAX = 2
ITERS = 4
CHUNKS = 2
MESH = pl.DeviceIdType.MESH


def merge_kernel(ops_in, ops_out, count, blocks, dense, sums, merged, last):
    slots, bs = blocks.shape[0], blocks.shape[1]
    nb, ni = dense.shape[0] // bs, dense.shape[1] // bs
    live = count[0, 0]

    def clear(cell, carry):
        last[cell] = slots
        return carry

    lax.fori_loop(0, nb * ni + 1, clear, 0, unroll=8)
    sums[slots] = jnp.zeros((bs, bs), jnp.float32)
    merged[slots] = jnp.zeros((bs, bs), merged.dtype)

    def add(s, carry):
        cell = jnp.where(s < live, ops_out[0, s] * ni + ops_in[0, s], nb * ni)
        total = sums[last[cell]] + blocks[s].astype(jnp.float32)
        last[cell] = s
        sums[s] = total
        merged[s] = total.astype(merged.dtype)
        return carry

    lax.fori_loop(0, slots, add, 0, unroll=4)

    def fill(j, carry):
        for i in range(ni):
            at = i - FX if FX <= i < FX + nb else (nb + i if i < FX else i)
            dense[pl.ds(j * bs, bs), at * bs : (at + 1) * bs] = merged[last[j * ni + i]]
        return carry

    lax.fori_loop(0, nb, fill, 0)


def sweep_kernel(
    sizes, source, dense, ups, downs, result,
    trace, faces_in, edges_in, up_pick, down_pick, own_sum, final,
    load_sem, store_sem, send_sem, recv_sem,
):
    n_gx, n_gy = sizes
    nb, bs, width = trace.shape[2:]
    rows, face, edge = nb * bs, FX * bs, EMAX * bs
    gx, gy = lax.axis_index("gx"), lax.axis_index("gy")
    right = (lax.rem(gx + 1, n_gx), gy)
    left = (lax.rem(gx + n_gx - 1, n_gx), gy)
    above = (gx, lax.rem(gy + 1, n_gy))
    below = (gx, lax.rem(gy + n_gy - 1, n_gy))
    has_above, has_below = gy < n_gy - 1, gy > 0

    barrier = pltpu.get_barrier_semaphore()
    for place in (right, left):
        pl.semaphore_signal(barrier, inc=1, device_id=place, device_id_type=MESH)

    @pl.when(has_above)
    def _():
        pl.semaphore_signal(barrier, inc=1, device_id=above, device_id_type=MESH)

    @pl.when(has_below)
    def _():
        pl.semaphore_signal(barrier, inc=1, device_id=below, device_id_type=MESH)

    loads = [
        pltpu.make_async_copy(
            source.at[:, :, pl.ds(c * width, width)], trace.at[0, c], load_sem.at[c]
        )
        for c in range(CHUNKS)
    ]
    for copy in loads:
        copy.start()

    @pl.when(jnp.logical_not(has_below))
    def _():
        edges_in[:, :, 0:EMAX] = jnp.zeros((ITERS, CHUNKS, EMAX, bs, width), edges_in.dtype)

    @pl.when(jnp.logical_not(has_above))
    def _():
        edges_in[:, :, EMAX:] = jnp.zeros((ITERS, CHUNKS, EMAX, bs, width), edges_in.dtype)

    def remote(t, c, which):
        src, dst, place = (
            (trace.at[t, c, pl.ds(nb - FX, FX)], faces_in.at[t, c, pl.ds(0, FX)], right),
            (trace.at[t, c, pl.ds(0, FX)], faces_in.at[t, c, pl.ds(FX, FX)], left),
            (up_pick.at[t, c], edges_in.at[t, c, pl.ds(0, EMAX)], above),
            (down_pick.at[t, c], edges_in.at[t, c, pl.ds(EMAX, EMAX)], below),
        )[which]
        return pltpu.make_async_remote_copy(
            src_ref=src,
            dst_ref=dst,
            send_sem=send_sem.at[t, c, which],
            recv_sem=recv_sem.at[t, c, which],
            device_id=place,
            device_id_type=MESH,
        )

    def send_edges(t, c):
        @pl.when(has_above)
        def _():
            for k in range(EMAX):
                up_pick[t, c, k] = trace[t, c, ups[0, k]]
            remote(t, c, 2).start()

        @pl.when(has_below)
        def _():
            for k in range(EMAX):
                down_pick[t, c, k] = trace[t, c, downs[0, k]]
            remote(t, c, 3).start()

    def dot(first_row, end_row, first, size, inputs):
        return jnp.dot(
            dense[first_row:end_row, first : first + size],
            inputs.reshape(size, width),
            preferred_element_type=jnp.float32,
        )

    def own_term(t, c):
        terms = trace[0, c].reshape(rows, width).astype(jnp.float32)
        own_sum[c] = terms + dot(0, rows, 0, rows, trace[t, c])

    for copy in loads:
        copy.wait()
    pl.semaphore_wait(barrier, 2 + has_above.astype(jnp.int32) + has_below.astype(jnp.int32))
    for c in range(CHUNKS):
        remote(0, c, 0).start()
        remote(0, c, 1).start()
        send_edges(0, c)
    for c in range(CHUNKS):
        own_term(0, c)

    for t in range(ITERS):
        for c in range(CHUNKS):
            @pl.when(has_below)
            def _():
                remote(t, c, 2).wait_recv()

            @pl.when(has_above)
            def _():
                remote(t, c, 3).wait_recv()

            own_sum[c] += dot(0, rows, rows + 2 * face, 2 * edge, edges_in[t, c])
            remote(t, c, 0).wait_recv()
            remote(t, c, 1).wait_recv()

            def finish(first_row, end_row):
                total = own_sum[c, first_row:end_row] + dot(
                    first_row, end_row, rows, 2 * face, faces_in[t, c]
                )
                value = total.astype(trace.dtype)
                if t == ITERS - 1:
                    final[c, first_row:end_row] = value
                else:
                    blocks = (end_row - first_row) // bs
                    trace[t + 1, c, first_row // bs : end_row // bs] = value.reshape(blocks, bs, width)

            if t == ITERS - 1:
                finish(0, rows)
                pltpu.make_async_copy(
                    final.at[c], result.at[:, pl.ds(c * width, width)], store_sem.at[c]
                ).start()
            else:
                finish(rows - face, rows)
                remote(t + 1, c, 0).start()
                finish(0, face)
                remote(t + 1, c, 1).start()
                finish(face, rows - face)
                send_edges(t + 1, c)
                own_term(t + 1, c)

    for t in range(ITERS):
        for c in range(CHUNKS):
            remote(t, c, 0).wait_send()
            remote(t, c, 1).wait_send()

            @pl.when(has_above)
            def _():
                remote(t, c, 2).wait_send()

            @pl.when(has_below)
            def _():
                remote(t, c, 3).wait_send()

    for c in range(CHUNKS):
        pltpu.make_async_copy(
            final.at[c], result.at[:, pl.ds(c * width, width)], store_sem.at[c]
        ).wait()


def shards(sizes, source, op_blocks, op_in, op_out, op_count, edge_up, edge_down):
    rows, columns = source.shape[2:]
    bs = op_blocks.shape[3]
    slots = op_in.shape[2]
    nb = rows // bs
    ni = nb + 2 * FX + 2 * EMAX
    width = columns // CHUNKS
    bf16 = jnp.bfloat16
    in_vmem = pl.BlockSpec(memory_space=pltpu.VMEM)
    in_smem = pl.BlockSpec(memory_space=pltpu.SMEM)
    anywhere = pl.BlockSpec(memory_space=pl.ANY)
    dense = pl.pallas_call(
        merge_kernel,
        out_shape=jax.ShapeDtypeStruct((rows, ni * bs), bf16),
        in_specs=[in_smem] * 3 + [in_vmem],
        out_specs=in_vmem,
        scratch_shapes=[
            pltpu.VMEM((slots + 1, bs, bs), jnp.float32),
            pltpu.VMEM((slots + 1, bs, bs), bf16),
            pltpu.SMEM((nb * ni + 1,), jnp.int32),
        ],
        compiler_params=pltpu.CompilerParams(vmem_limit_bytes=32 * 1024 * 1024),
    )(op_in.reshape(1, slots), op_out.reshape(1, slots), op_count, op_blocks.reshape(slots, bs, bs))
    out = pl.pallas_call(
        functools.partial(sweep_kernel, sizes),
        out_shape=jax.ShapeDtypeStruct((rows, columns), bf16),
        in_specs=[anywhere, in_vmem, in_smem, in_smem],
        out_specs=anywhere,
        scratch_shapes=[
            pltpu.VMEM((ITERS, CHUNKS, nb, bs, width), bf16),
            pltpu.VMEM((ITERS, CHUNKS, 2 * FX, bs, width), bf16),
            pltpu.VMEM((ITERS, CHUNKS, 2 * EMAX, bs, width), bf16),
            pltpu.VMEM((ITERS, CHUNKS, EMAX, bs, width), bf16),
            pltpu.VMEM((ITERS, CHUNKS, EMAX, bs, width), bf16),
            pltpu.VMEM((CHUNKS, rows, width), jnp.float32),
            pltpu.VMEM((CHUNKS, rows, width), bf16),
            pltpu.SemaphoreType.DMA((CHUNKS,)),
            pltpu.SemaphoreType.DMA((CHUNKS,)),
            pltpu.SemaphoreType.DMA((ITERS, CHUNKS, 4)),
            pltpu.SemaphoreType.DMA((ITERS, CHUNKS, 4)),
        ],
        compiler_params=pltpu.CompilerParams(
            collective_id=0, has_side_effects=True, vmem_limit_bytes=32 * 1024 * 1024
        ),
    )(source.reshape(nb, bs, columns), dense, edge_up.reshape(1, EMAX), edge_down.reshape(1, EMAX))
    return out.reshape(source.shape)


def solution(mesh):
    placed = (
        P("gx", "gy", None, None),
        P("gx", "gy", None, None),
        P("gx", "gy", None),
        P("gx", "gy", None),
        P("gx", "gy"),
        P("gx", "gy", None),
        P("gx", "gy", None),
    )
    sizes = (mesh.shape["gx"], mesh.shape["gy"])
    return jax.shard_map(
        functools.partial(shards, sizes),
        mesh=mesh,
        in_specs=placed,
        out_specs=P("gx", "gy", None, None),
        check_vma=False,
    )
```

```python
import functools

import jax
import jax.numpy as jnp
from jax import lax
from jax.experimental import pallas as pl
from jax.experimental.pallas import tpu as pltpu
from jax.sharding import PartitionSpec as P

FX = 2
EMAX = 2
ITERS = 4
CHUNKS = 2
VMEM_LIMIT = 60 * 1024 * 1024
MESH = pl.DeviceIdType.MESH


LANES = 128
STRIDE = 32


def slot_table(in_row, out_row, count, table, slots, nb, ni):
    lanes = lax.broadcasted_iota(jnp.int32, (LANES, LANES), 1)
    subs = lax.broadcasted_iota(jnp.int32, (LANES, LANES), 0)
    row_ids = lax.broadcasted_iota(jnp.int32, (1, LANES), 1)
    is_own = (in_row >= FX) & (in_row < FX + nb)
    place = jnp.where(in_row < FX, in_row + nb, jnp.where(is_own, in_row - FX, in_row))
    cell_row = jnp.where(row_ids < count, place * STRIDE + out_row, 1 << 20)
    cells_t = jnp.broadcast_to(cell_row, (LANES, LANES))
    cells_s = jnp.broadcast_to(
        jnp.sum(jnp.where(lanes == subs, cells_t, 0), axis=1, keepdims=True), (LANES, LANES)
    )
    before = (cells_t < cells_s) | ((cells_t == cells_s) & (lanes < subs))
    rank = jnp.broadcast_to(
        jnp.sum(jnp.where(before, 1, 0), axis=1, keepdims=True), (LANES, LANES)
    )
    perm = jnp.sum(jnp.where(rank == lanes, subs, 0), axis=0, keepdims=True)
    here = jnp.sum(jnp.where(rank == lanes, cells_s, 0), axis=0, keepdims=True)
    previous = jnp.sum(jnp.where(rank + 1 == lanes, cells_s, 0), axis=0, keepdims=True)
    table[0:1, :] = jnp.minimum(perm, slots - 1)
    table[1:2, :] = jnp.where((row_ids > 0) & (here == previous), 1, 0)
    for part in range(-(-ni * STRIDE // LANES)):
        wanted = lanes + part * LANES
        upto = jnp.sum(jnp.where(cells_s <= wanted, 1, 0), axis=0, keepdims=True)
        equal = jnp.sum(jnp.where(cells_s == wanted, 1, 0), axis=0, keepdims=True)
        table[2 + part : 3 + part, :] = jnp.where(equal > 0, upto - 1, slots)


def sweep_kernel(
    sizes, source, blocks, ops_in, ops_out, count, ups, downs, result,
    raw, trace, faces_in, edges_in, up_pick, down_pick, own_sum, final,
    ops, merged, dense, in_row, out_row, table, places,
    load_sem, table_sem, store_sem, send_sem, recv_sem,
):
    n_gx, n_gy = sizes
    nb, width, bs = trace.shape[2:]
    slots, ni = blocks.shape[0], dense.shape[0] // bs
    gx, gy = lax.axis_index("gx"), lax.axis_index("gy")
    right = (lax.rem(gx + 1, n_gx), gy)
    left = (lax.rem(gx + n_gx - 1, n_gx), gy)
    above = (gx, lax.rem(gy + 1, n_gy))
    below = (gx, lax.rem(gy + n_gy - 1, n_gy))
    has_above, has_below = gy < n_gy - 1, gy > 0

    barrier = pltpu.get_barrier_semaphore()
    for place in (right, left):
        pl.semaphore_signal(barrier, inc=1, device_id=place, device_id_type=MESH)

    @pl.when(has_above)
    def _():
        pl.semaphore_signal(barrier, inc=1, device_id=above, device_id_type=MESH)

    @pl.when(has_below)
    def _():
        pl.semaphore_signal(barrier, inc=1, device_id=below, device_id_type=MESH)

    loads = [
        pltpu.make_async_copy(
            source.at[:, :, pl.ds(c * width, width)], raw.at[c], load_sem.at[c]
        )
        for c in range(CHUNKS)
    ]
    ops_load = pltpu.make_async_copy(blocks, ops, load_sem.at[CHUNKS])
    for copy in loads + [ops_load]:
        copy.start()

    in_row[...] = jnp.zeros_like(in_row)
    out_row[...] = jnp.zeros_like(out_row)
    in_row[:, 0:slots] = ops_in[...]
    out_row[:, 0:slots] = ops_out[...]
    slot_table(in_row[...], out_row[...], count[0, 0], table, slots, nb, ni)
    table_copy = pltpu.make_async_copy(table, places, table_sem)
    table_copy.start()

    @pl.when(jnp.logical_not(has_below))
    def _():
        edges_in[:, :, 0:EMAX] = jnp.zeros((ITERS, CHUNKS, EMAX, width, bs), edges_in.dtype)

    @pl.when(jnp.logical_not(has_above))
    def _():
        edges_in[:, :, EMAX:] = jnp.zeros((ITERS, CHUNKS, EMAX, width, bs), edges_in.dtype)

    def remote(t, c, which):
        src, dst, place = (
            (trace.at[t, c, pl.ds(nb - FX, FX)], faces_in.at[t, c, pl.ds(0, FX)], right),
            (trace.at[t, c, pl.ds(0, FX)], faces_in.at[t, c, pl.ds(FX, FX)], left),
            (up_pick.at[t, c], edges_in.at[t, c, pl.ds(0, EMAX)], above),
            (down_pick.at[t, c], edges_in.at[t, c, pl.ds(EMAX, EMAX)], below),
        )[which]
        return pltpu.make_async_remote_copy(
            src_ref=src,
            dst_ref=dst,
            send_sem=send_sem.at[t, c, which],
            recv_sem=recv_sem.at[t, c, which],
            device_id=place,
            device_id_type=MESH,
        )

    def send_edges(t, c):
        @pl.when(has_above)
        def _():
            for k in range(EMAX):
                up_pick[t, c, k] = trace[t, c, ups[0, k]]
            remote(t, c, 2).start()

        @pl.when(has_below)
        def _():
            for k in range(EMAX):
                down_pick[t, c, k] = trace[t, c, downs[0, k]]
            remote(t, c, 3).start()

    def side_by_side(ref, t, c, count):
        return jnp.concatenate([ref[t, c, j] for j in range(count)], axis=1)

    def dot(inputs, first, end, first_out, end_out):
        return jnp.dot(
            inputs,
            dense[first * bs : end * bs, first_out * bs : end_out * bs],
            preferred_element_type=jnp.float32,
        )

    def own_term(t, c):
        terms = side_by_side(trace, 0, c, nb).astype(jnp.float32)
        own_sum[c] = terms + dot(side_by_side(trace, t, c, nb), 0, nb, 0, nb)

    waited = False
    for c in range(CHUNKS):
        loads[c].wait()
        for j in range(nb):
            trace[0, c, j] = raw[c, j].astype(jnp.float32).T.astype(trace.dtype)
        if not waited:
            pl.semaphore_wait(
                barrier, 2 + has_above.astype(jnp.int32) + has_below.astype(jnp.int32)
            )
            waited = True
        remote(0, c, 0).start()
        remote(0, c, 1).start()
        send_edges(0, c)

    table_copy.wait()
    ops_load.wait()
    merged[slots] = jnp.zeros((bs, bs), merged.dtype)

    def merge(p, total):
        total = jnp.where(places[1, p] > 0, total, 0.0) + ops[places[0, p]].astype(jnp.float32)
        merged[p] = total.T.astype(merged.dtype)
        return total

    lax.fori_loop(0, slots, merge, jnp.zeros((bs, bs), jnp.float32), unroll=4)
    for i in range(ni):
        for j in range(nb):
            cell = i * STRIDE + j
            dense[i * bs : (i + 1) * bs, j * bs : (j + 1) * bs] = merged[
                places[2 + cell // LANES, cell % LANES]
            ]
    for c in range(CHUNKS):
        own_term(0, c)

    for t in range(ITERS):
        for c in range(CHUNKS):
            @pl.when(has_below)
            def _():
                remote(t, c, 2).wait_recv()

            @pl.when(has_above)
            def _():
                remote(t, c, 3).wait_recv()

            own_sum[c] += dot(
                side_by_side(edges_in, t, c, 2 * EMAX), nb + 2 * FX, ni, 0, nb
            )
            remote(t, c, 0).wait_recv()
            remote(t, c, 1).wait_recv()

            faces = side_by_side(faces_in, t, c, 2 * FX)

            def finish(first, end):
                total = own_sum[c, :, first * bs : end * bs] + dot(
                    faces, nb, nb + 2 * FX, first, end
                )
                if t == ITERS - 1:
                    final[c] = total.T.astype(final.dtype)
                else:
                    for j in range(first, end):
                        trace[t + 1, c, j] = total[:, (j - first) * bs : (j - first + 1) * bs].astype(
                            trace.dtype
                        )

            if t == ITERS - 1:
                finish(0, nb)
                pltpu.make_async_copy(
                    final.at[c], result.at[:, pl.ds(c * width, width)], store_sem.at[c]
                ).start()
            else:
                finish(nb - FX, nb)
                remote(t + 1, c, 0).start()
                finish(0, FX)
                remote(t + 1, c, 1).start()
                finish(FX, nb - FX)
                send_edges(t + 1, c)
                own_term(t + 1, c)

    for t in range(ITERS):
        for c in range(CHUNKS):
            remote(t, c, 0).wait_send()
            remote(t, c, 1).wait_send()

            @pl.when(has_above)
            def _():
                remote(t, c, 2).wait_send()

            @pl.when(has_below)
            def _():
                remote(t, c, 3).wait_send()

    for c in range(CHUNKS):
        pltpu.make_async_copy(
            final.at[c], result.at[:, pl.ds(c * width, width)], store_sem.at[c]
        ).wait()


def shards(sizes, source, op_blocks, op_in, op_out, op_count, edge_up, edge_down):
    rows, columns = source.shape[2:]
    bs = op_blocks.shape[3]
    slots = op_in.shape[2]
    nb = rows // bs
    ni = nb + 2 * FX + 2 * EMAX
    width = columns // CHUNKS
    bf16 = jnp.bfloat16
    in_vmem = pl.BlockSpec(memory_space=pltpu.VMEM)
    in_smem = pl.BlockSpec(memory_space=pltpu.SMEM)
    anywhere = pl.BlockSpec(memory_space=pl.ANY)
    out = pl.pallas_call(
        functools.partial(sweep_kernel, sizes),
        out_shape=jax.ShapeDtypeStruct((rows, columns), bf16),
        in_specs=[anywhere] * 2 + [in_vmem] * 2 + [in_smem] * 3,
        out_specs=anywhere,
        scratch_shapes=[
            pltpu.VMEM((CHUNKS, nb, bs, width), bf16),
            pltpu.VMEM((ITERS, CHUNKS, nb, width, bs), bf16),
            pltpu.VMEM((ITERS, CHUNKS, 2 * FX, width, bs), bf16),
            pltpu.VMEM((ITERS, CHUNKS, 2 * EMAX, width, bs), bf16),
            pltpu.VMEM((ITERS, CHUNKS, EMAX, width, bs), bf16),
            pltpu.VMEM((ITERS, CHUNKS, EMAX, width, bs), bf16),
            pltpu.VMEM((CHUNKS, width, rows), jnp.float32),
            pltpu.VMEM((CHUNKS, rows, width), bf16),
            pltpu.VMEM((slots, bs, bs), bf16),
            pltpu.VMEM((slots + 1, bs, bs), bf16),
            pltpu.VMEM((ni * bs, rows), bf16),
            pltpu.VMEM((1, LANES), jnp.int32),
            pltpu.VMEM((1, LANES), jnp.int32),
            pltpu.VMEM((8, LANES), jnp.int32),
            pltpu.SMEM((8, LANES), jnp.int32),
            pltpu.SemaphoreType.DMA((CHUNKS + 1,)),
            pltpu.SemaphoreType.DMA,
            pltpu.SemaphoreType.DMA((CHUNKS,)),
            pltpu.SemaphoreType.DMA((ITERS, CHUNKS, 4)),
            pltpu.SemaphoreType.DMA((ITERS, CHUNKS, 4)),
        ],
        compiler_params=pltpu.CompilerParams(
            collective_id=0, has_side_effects=True, vmem_limit_bytes=VMEM_LIMIT
        ),
    )(
        source.reshape(nb, bs, columns),
        op_blocks.reshape(slots, bs, bs),
        op_in.reshape(1, slots),
        op_out.reshape(1, slots),
        op_count,
        edge_up.reshape(1, EMAX),
        edge_down.reshape(1, EMAX),
    )
    return out.reshape(source.shape)


def solution(mesh):
    placed = (
        P("gx", "gy", None, None),
        P("gx", "gy", None, None),
        P("gx", "gy", None),
        P("gx", "gy", None),
        P("gx", "gy"),
        P("gx", "gy", None),
        P("gx", "gy", None),
    )
    sizes = (mesh.shape["gx"], mesh.shape["gy"])
    return jax.shard_map(
        functools.partial(shards, sizes),
        mesh=mesh,
        in_specs=placed,
        out_specs=P("gx", "gy", None, None),
        check_vma=False,
    )
```

```python
import functools

import jax
import jax.numpy as jnp
from jax import lax
from jax.experimental import pallas as pl
from jax.experimental.pallas import tpu as pltpu
from jax.sharding import PartitionSpec as P

FX = 2
EMAX = 2
ITERS = 4
CHUNKS = 2
VMEM_LIMIT = 58 * 1024 * 1024
MESH = pl.DeviceIdType.MESH


LANES = 128
STRIDE = 32


def slot_table(in_row, out_row, count, table, slots, nb, ni):
    lanes = lax.broadcasted_iota(jnp.int32, (LANES, LANES), 1)
    subs = lax.broadcasted_iota(jnp.int32, (LANES, LANES), 0)
    row_ids = lax.broadcasted_iota(jnp.int32, (1, LANES), 1)
    is_own = (in_row >= FX) & (in_row < FX + nb)
    place = jnp.where(in_row < FX, in_row + nb, jnp.where(is_own, in_row - FX, in_row))
    cell_row = jnp.where(row_ids < count, place * STRIDE + out_row, 1 << 20)
    cells_t = jnp.broadcast_to(cell_row, (LANES, LANES))
    cells_s = jnp.broadcast_to(
        jnp.sum(jnp.where(lanes == subs, cells_t, 0), axis=1, keepdims=True), (LANES, LANES)
    )
    before = (cells_t < cells_s) | ((cells_t == cells_s) & (lanes < subs))
    rank = jnp.broadcast_to(
        jnp.sum(jnp.where(before, 1, 0), axis=1, keepdims=True), (LANES, LANES)
    )
    perm = jnp.sum(jnp.where(rank == lanes, subs, 0), axis=0, keepdims=True)
    here = jnp.sum(jnp.where(rank == lanes, cells_s, 0), axis=0, keepdims=True)
    previous = jnp.sum(jnp.where(rank + 1 == lanes, cells_s, 0), axis=0, keepdims=True)
    table[0:1, :] = jnp.minimum(perm, slots - 1)
    table[1:2, :] = jnp.where((row_ids > 0) & (here == previous), 1, 0)
    for part in range(-(-ni * STRIDE // LANES)):
        wanted = lanes + part * LANES
        upto = jnp.sum(jnp.where(cells_s <= wanted, 1, 0), axis=0, keepdims=True)
        equal = jnp.sum(jnp.where(cells_s == wanted, 1, 0), axis=0, keepdims=True)
        table[2 + part : 3 + part, :] = jnp.where(equal > 0, upto - 1, slots)


def sweep_kernel(
    sizes, source, blocks, ops_in, ops_out, count, ups_in, downs_in, result,
    raw, trace, faces_in, edges_in, up_pick, down_pick, own_sum,
    ops, merged, dense, in_list, out_list, in_row, out_row, table, places, ups, downs,
    load_sem, small_sem, table_sem, send_sem, recv_sem,
):
    n_gx, n_gy = sizes
    nb, width, bs = trace.shape[2:]
    slots, ni = blocks.shape[0], dense.shape[0] // bs
    gx, gy = lax.axis_index("gx"), lax.axis_index("gy")
    right = (lax.rem(gx + 1, n_gx), gy)
    left = (lax.rem(gx + n_gx - 1, n_gx), gy)
    above = (gx, lax.rem(gy + 1, n_gy))
    below = (gx, lax.rem(gy + n_gy - 1, n_gy))
    has_above, has_below = gy < n_gy - 1, gy > 0

    barrier = pltpu.get_barrier_semaphore()
    for place in (right, left):
        pl.semaphore_signal(barrier, inc=1, device_id=place, device_id_type=MESH)

    @pl.when(has_above)
    def _():
        pl.semaphore_signal(barrier, inc=1, device_id=above, device_id_type=MESH)

    @pl.when(has_below)
    def _():
        pl.semaphore_signal(barrier, inc=1, device_id=below, device_id_type=MESH)

    loads = [
        pltpu.make_async_copy(
            source.at[:, :, pl.ds(c * width, width)], raw.at[c], load_sem.at[c]
        )
        for c in range(CHUNKS)
    ]
    ops_load = pltpu.make_async_copy(blocks, ops, load_sem.at[CHUNKS])
    pairs = ((ops_in, in_list), (ops_out, out_list), (ups_in, ups), (downs_in, downs))
    small = [
        pltpu.make_async_copy(src, dst, small_sem.at[k]) for k, (src, dst) in enumerate(pairs)
    ]
    for copy in loads + small:
        copy.start()

    in_row[...] = jnp.zeros_like(in_row)
    out_row[...] = jnp.zeros_like(out_row)
    for copy in small:
        copy.wait()
    in_row[:, 0:slots] = in_list[...]
    out_row[:, 0:slots] = out_list[...]
    slot_table(in_row[...], out_row[...], count[0, 0], table, slots, nb, ni)
    table_copy = pltpu.make_async_copy(table, places, table_sem)
    table_copy.start()

    @pl.when(jnp.logical_not(has_below))
    def _():
        edges_in[:, :, 0:EMAX] = jnp.zeros((ITERS, CHUNKS, EMAX, width, bs), edges_in.dtype)

    @pl.when(jnp.logical_not(has_above))
    def _():
        edges_in[:, :, EMAX:] = jnp.zeros((ITERS, CHUNKS, EMAX, width, bs), edges_in.dtype)

    def remote(t, c, which):
        src, dst, place = (
            (trace.at[t, c, pl.ds(nb - FX, FX)], faces_in.at[t, c, pl.ds(0, FX)], right),
            (trace.at[t, c, pl.ds(0, FX)], faces_in.at[t, c, pl.ds(FX, FX)], left),
            (up_pick.at[t, c], edges_in.at[t, c, pl.ds(0, EMAX)], above),
            (down_pick.at[t, c], edges_in.at[t, c, pl.ds(EMAX, EMAX)], below),
        )[which]
        return pltpu.make_async_remote_copy(
            src_ref=src,
            dst_ref=dst,
            send_sem=send_sem.at[t, c, which],
            recv_sem=recv_sem.at[t, c, which],
            device_id=place,
            device_id_type=MESH,
        )

    def send_edges(t, c):
        @pl.when(has_above)
        def _():
            for k in range(EMAX):
                up_pick[t, c, k] = trace[t, c, ups[0, k]]
            remote(t, c, 2).start()

        @pl.when(has_below)
        def _():
            for k in range(EMAX):
                down_pick[t, c, k] = trace[t, c, downs[0, k]]
            remote(t, c, 3).start()

    def side_by_side(ref, t, c, count):
        return jnp.concatenate([ref[t, c, j] for j in range(count)], axis=1)

    def dot(inputs, first, end, first_out, end_out):
        return jnp.dot(
            inputs,
            dense[first * bs : end * bs, first_out * bs : end_out * bs],
            preferred_element_type=jnp.float32,
        )

    def own_term(t, c):
        terms = side_by_side(trace, 0, c, nb).astype(jnp.float32)
        own_sum[c] = terms + dot(side_by_side(trace, t, c, nb), 0, nb, 0, nb)

    for c in range(CHUNKS):
        loads[c].wait()
        for j in (*range(nb - FX, nb), *range(nb - FX)):
            trace[0, c, j] = raw[c, j].astype(jnp.float32).T.astype(trace.dtype)
            if j == FX - 1:
                if c == 0:
                    pl.semaphore_wait(
                        barrier, 2 + has_above.astype(jnp.int32) + has_below.astype(jnp.int32)
                    )
                remote(0, c, 0).start()
                remote(0, c, 1).start()
        send_edges(0, c)
    ops_load.start()

    table_copy.wait()
    ops_load.wait()
    merged[slots] = jnp.zeros((bs, bs), merged.dtype)

    def merge(p, total):
        total = jnp.where(places[1, p] > 0, total, 0.0) + ops[places[0, p]].astype(jnp.float32)
        merged[p] = total.T.astype(merged.dtype)
        return total

    lax.fori_loop(0, slots, merge, jnp.zeros((bs, bs), jnp.float32), unroll=4)
    for i in range(ni):
        for j in range(nb):
            cell = i * STRIDE + j
            dense[i * bs : (i + 1) * bs, j * bs : (j + 1) * bs] = merged[
                places[2 + cell // LANES, cell % LANES]
            ]
    for c in range(CHUNKS):
        own_term(0, c)

    for t in range(ITERS):
        for c in range(CHUNKS):
            @pl.when(has_below)
            def _():
                remote(t, c, 2).wait_recv()

            @pl.when(has_above)
            def _():
                remote(t, c, 3).wait_recv()

            own_sum[c] += dot(
                side_by_side(edges_in, t, c, 2 * EMAX), nb + 2 * FX, ni, 0, nb
            )
            remote(t, c, 0).wait_recv()
            remote(t, c, 1).wait_recv()

            faces = side_by_side(faces_in, t, c, 2 * FX)

            def finish(first, end):
                total = own_sum[c, :, first * bs : end * bs] + dot(
                    faces, nb, nb + 2 * FX, first, end
                )
                if t == ITERS - 1:
                    result[:, c * width : (c + 1) * width] = total.T.astype(result.dtype)
                else:
                    for j in range(first, end):
                        trace[t + 1, c, j] = total[:, (j - first) * bs : (j - first + 1) * bs].astype(
                            trace.dtype
                        )

            if t == ITERS - 1:
                finish(0, nb)
            else:
                finish(nb - FX, nb)
                remote(t + 1, c, 0).start()
                finish(0, FX)
                remote(t + 1, c, 1).start()
                finish(FX, nb - FX)
                send_edges(t + 1, c)
                own_term(t + 1, c)

    for t in range(ITERS):
        for c in range(CHUNKS):
            remote(t, c, 0).wait_send()
            remote(t, c, 1).wait_send()

            @pl.when(has_above)
            def _():
                remote(t, c, 2).wait_send()

            @pl.when(has_below)
            def _():
                remote(t, c, 3).wait_send()


def shards(sizes, source, op_blocks, op_in, op_out, op_count, edge_up, edge_down):
    rows, columns = source.shape[2:]
    bs = op_blocks.shape[3]
    slots = op_in.shape[2]
    nb = rows // bs
    ni = nb + 2 * FX + 2 * EMAX
    width = columns // CHUNKS
    bf16 = jnp.bfloat16
    in_smem = pl.BlockSpec(memory_space=pltpu.SMEM)
    in_vmem = pl.BlockSpec(memory_space=pltpu.VMEM)
    anywhere = pl.BlockSpec(memory_space=pl.ANY)
    out = pl.pallas_call(
        functools.partial(sweep_kernel, sizes),
        out_shape=pltpu.VMEM((rows, columns), bf16),
        in_specs=[anywhere] * 4 + [in_smem] + [anywhere] * 2,
        out_specs=in_vmem,
        scratch_shapes=[
            pltpu.VMEM((CHUNKS, nb, bs, width), bf16),
            pltpu.VMEM((ITERS, CHUNKS, nb, width, bs), bf16),
            pltpu.VMEM((ITERS, CHUNKS, 2 * FX, width, bs), bf16),
            pltpu.VMEM((ITERS, CHUNKS, 2 * EMAX, width, bs), bf16),
            pltpu.VMEM((ITERS, CHUNKS, EMAX, width, bs), bf16),
            pltpu.VMEM((ITERS, CHUNKS, EMAX, width, bs), bf16),
            pltpu.VMEM((CHUNKS, width, rows), jnp.float32),
            pltpu.VMEM((slots, bs, bs), bf16),
            pltpu.VMEM((slots + 1, bs, bs), bf16),
            pltpu.VMEM((ni * bs, rows), bf16),
            pltpu.VMEM((1, slots), jnp.int32),
            pltpu.VMEM((1, slots), jnp.int32),
            pltpu.VMEM((1, LANES), jnp.int32),
            pltpu.VMEM((1, LANES), jnp.int32),
            pltpu.VMEM((8, LANES), jnp.int32),
            pltpu.SMEM((8, LANES), jnp.int32),
            pltpu.SMEM((1, EMAX), jnp.int32),
            pltpu.SMEM((1, EMAX), jnp.int32),
            pltpu.SemaphoreType.DMA((CHUNKS + 1,)),
            pltpu.SemaphoreType.DMA((4,)),
            pltpu.SemaphoreType.DMA,
            pltpu.SemaphoreType.DMA((ITERS, CHUNKS, 4)),
            pltpu.SemaphoreType.DMA((ITERS, CHUNKS, 4)),
        ],
        compiler_params=pltpu.CompilerParams(
            collective_id=0, has_side_effects=True, vmem_limit_bytes=VMEM_LIMIT
        ),
    )(
        source.reshape(nb, bs, columns),
        op_blocks.reshape(slots, bs, bs),
        op_in.reshape(1, slots),
        op_out.reshape(1, slots),
        op_count,
        edge_up.reshape(1, EMAX),
        edge_down.reshape(1, EMAX),
    )
    return out.reshape(source.shape)


def solution(mesh):
    placed = (
        P("gx", "gy", None, None),
        P("gx", "gy", None, None),
        P("gx", "gy", None),
        P("gx", "gy", None),
        P("gx", "gy"),
        P("gx", "gy", None),
        P("gx", "gy", None),
    )
    sizes = (mesh.shape["gx"], mesh.shape["gy"])
    return jax.shard_map(
        functools.partial(shards, sizes),
        mesh=mesh,
        in_specs=placed,
        out_specs=P("gx", "gy", None, None),
        check_vma=False,
    )
```

```python
import functools

import jax
import jax.numpy as jnp
from jax import lax
from jax.experimental import pallas as pl
from jax.experimental.pallas import tpu as pltpu
from jax.sharding import PartitionSpec as P

FX = 2
EMAX = 2
ITERS = 4
CHUNKS = 2
VMEM_LIMIT = 58 * 1024 * 1024
RELAYS = {(0, 1): 0, (1, 0): 2, (1, 1): 4}
MESH = pl.DeviceIdType.MESH


LANES = 128
STRIDE = 32


def slot_table(in_row, out_row, count, table, slots, nb, ni):
    lanes = lax.broadcasted_iota(jnp.int32, (LANES, LANES), 1)
    subs = lax.broadcasted_iota(jnp.int32, (LANES, LANES), 0)
    row_ids = lax.broadcasted_iota(jnp.int32, (1, LANES), 1)
    is_own = (in_row >= FX) & (in_row < FX + nb)
    place = jnp.where(in_row < FX, in_row + nb, jnp.where(is_own, in_row - FX, in_row))
    cell_row = jnp.where(row_ids < count, place * STRIDE + out_row, 1 << 20)
    cells_t = jnp.broadcast_to(cell_row, (LANES, LANES))
    cells_s = jnp.broadcast_to(
        jnp.sum(jnp.where(lanes == subs, cells_t, 0), axis=1, keepdims=True), (LANES, LANES)
    )
    before = (cells_t < cells_s) | ((cells_t == cells_s) & (lanes < subs))
    rank = jnp.broadcast_to(
        jnp.sum(jnp.where(before, 1, 0), axis=1, keepdims=True), (LANES, LANES)
    )
    perm = jnp.sum(jnp.where(rank == lanes, subs, 0), axis=0, keepdims=True)
    here = jnp.sum(jnp.where(rank == lanes, cells_s, 0), axis=0, keepdims=True)
    previous = jnp.sum(jnp.where(rank + 1 == lanes, cells_s, 0), axis=0, keepdims=True)
    table[0:1, :] = jnp.minimum(perm, slots - 1)
    table[1:2, :] = jnp.where((row_ids > 0) & (here == previous), 1, 0)
    for part in range(-(-ni * STRIDE // LANES)):
        wanted = lanes + part * LANES
        upto = jnp.sum(jnp.where(cells_s <= wanted, 1, 0), axis=0, keepdims=True)
        equal = jnp.sum(jnp.where(cells_s == wanted, 1, 0), axis=0, keepdims=True)
        table[2 + part : 3 + part, :] = jnp.where(equal > 0, upto - 1, slots)


def sweep_kernel(
    sizes, source, blocks, ops_in, ops_out, count, ups_in, downs_in, result,
    raw, trace, relay_in, faces_in, edges_in, up_pick, down_pick, own_sum,
    ops, merged, dense, in_list, out_list, in_row, out_row, table, places, ups, downs,
    load_sem, small_sem, table_sem, send_sem, recv_sem,
    cross_send, cross_recv, relay_send, relay_recv,
):
    n_gx, n_gy = sizes
    nb, width, bs = trace.shape[2:]
    slots, ni = blocks.shape[0], dense.shape[0] // bs
    gx, gy = lax.axis_index("gx"), lax.axis_index("gy")
    right = (lax.rem(gx + 1, n_gx), gy)
    left = (lax.rem(gx + n_gx - 1, n_gx), gy)
    above = (gx, lax.rem(gy + 1, n_gy))
    below = (gx, lax.rem(gy + n_gy - 1, n_gy))
    has_above, has_below = gy < n_gy - 1, gy > 0

    middle = n_gy // 2
    low, high = gy == middle - 1, gy == middle
    up_relays = sorted(RELAYS.values())
    down_relays = [n_gy - 1 - relay for relay in up_relays]
    is_relay = functools.reduce(jnp.logical_or, [gy == r for r in up_relays + down_relays])
    greeted = (
        2
        + has_above.astype(jnp.int32)
        + has_below.astype(jnp.int32)
        + 2 * is_relay.astype(jnp.int32)
        + 2 * len(RELAYS) * jnp.logical_or(low, high).astype(jnp.int32)
    )

    barrier = pltpu.get_barrier_semaphore()
    for place in (right, left):
        pl.semaphore_signal(barrier, inc=1, device_id=place, device_id_type=MESH)

    @pl.when(has_above)
    def _():
        pl.semaphore_signal(barrier, inc=1, device_id=above, device_id_type=MESH)

    @pl.when(has_below)
    def _():
        pl.semaphore_signal(barrier, inc=1, device_id=below, device_id_type=MESH)

    @pl.when(is_relay)
    def _():
        for end in (middle - 1, middle):
            pl.semaphore_signal(barrier, inc=1, device_id=(gx, end), device_id_type=MESH)

    @pl.when(jnp.logical_or(low, high))
    def _():
        for relay in up_relays + down_relays:
            pl.semaphore_signal(barrier, inc=1, device_id=(gx, relay), device_id_type=MESH)

    loads = [
        pltpu.make_async_copy(
            source.at[:, :, pl.ds(c * width, width)], raw.at[c], load_sem.at[c]
        )
        for c in range(CHUNKS)
    ]
    ops_load = pltpu.make_async_copy(blocks, ops, load_sem.at[CHUNKS])
    pairs = ((ops_in, in_list), (ops_out, out_list), (ups_in, ups), (downs_in, downs))
    small = [
        pltpu.make_async_copy(src, dst, small_sem.at[k]) for k, (src, dst) in enumerate(pairs)
    ]
    for copy in loads + small:
        copy.start()

    in_row[...] = jnp.zeros_like(in_row)
    out_row[...] = jnp.zeros_like(out_row)
    for copy in small:
        copy.wait()
    in_row[:, 0:slots] = in_list[...]
    out_row[:, 0:slots] = out_list[...]
    slot_table(in_row[...], out_row[...], count[0, 0], table, slots, nb, ni)
    table_copy = pltpu.make_async_copy(table, places, table_sem)
    table_copy.start()

    @pl.when(jnp.logical_not(has_below))
    def _():
        edges_in[:, :, 0:EMAX] = jnp.zeros((ITERS, CHUNKS, EMAX, width, bs), edges_in.dtype)

    @pl.when(jnp.logical_not(has_above))
    def _():
        edges_in[:, :, EMAX:] = jnp.zeros((ITERS, CHUNKS, EMAX, width, bs), edges_in.dtype)

    def remote(t, c, which):
        src, dst, place = (
            (trace.at[t, c, pl.ds(nb - FX, FX)], faces_in.at[t, c, pl.ds(0, FX)], right),
            (trace.at[t, c, pl.ds(0, FX)], faces_in.at[t, c, pl.ds(FX, FX)], left),
            (up_pick.at[t, c], edges_in.at[t, c, pl.ds(0, EMAX)], above),
            (down_pick.at[t, c], edges_in.at[t, c, pl.ds(EMAX, EMAX)], below),
        )[which]
        return pltpu.make_async_remote_copy(
            src_ref=src,
            dst_ref=dst,
            send_sem=send_sem.at[t, c, which],
            recv_sem=recv_sem.at[t, c, which],
            device_id=place,
            device_id_type=MESH,
        )

    ways = (
        (low, high, middle, up_pick, 0, lambda relay: relay),
        (high, low, middle - 1, down_pick, EMAX, lambda relay: n_gy - 1 - relay),
    )

    def crossing(way, t, c, k):
        _, _, end, pick, first, side = way
        relay = side(RELAYS[c, k]) if (c, k) in RELAYS else None
        return pltpu.make_async_remote_copy(
            src_ref=pick.at[t, c, k],
            dst_ref=edges_in.at[t, c, first + k] if relay is None else relay_in.at[t, c, k],
            send_sem=cross_send.at[t, c, k],
            recv_sem=cross_recv.at[t, c, k] if relay is None else relay_recv.at[t, c, k],
            device_id=(gx, end if relay is None else relay),
            device_id_type=MESH,
        )

    def onward(way, t, c, k):
        _, _, end, _, first, _ = way
        return pltpu.make_async_remote_copy(
            src_ref=relay_in.at[t, c, k],
            dst_ref=edges_in.at[t, c, first + k],
            send_sem=relay_send.at[t, c, k],
            recv_sem=cross_recv.at[t, c, k],
            device_id=(gx, end),
            device_id_type=MESH,
        )

    def forward(t, c):
        for (chunk, k), relay in RELAYS.items():
            if chunk == c:
                for way in ways:
                    @pl.when(gy == way[5](relay))
                    def _():
                        crossing(way, t, c, k).wait_recv()
                        onward(way, t, c, k).start()

    plain_above = jnp.logical_and(has_above, jnp.logical_not(low))
    plain_below = jnp.logical_and(has_below, jnp.logical_not(high))

    def send_edges(t, c):
        @pl.when(has_above)
        def _():
            for k in range(EMAX):
                up_pick[t, c, k] = trace[t, c, ups[0, k]]

        @pl.when(has_below)
        def _():
            for k in range(EMAX):
                down_pick[t, c, k] = trace[t, c, downs[0, k]]

        @pl.when(plain_above)
        def _():
            remote(t, c, 2).start()

        @pl.when(plain_below)
        def _():
            remote(t, c, 3).start()

        for way in ways:
            @pl.when(way[0])
            def _():
                for k in range(EMAX):
                    crossing(way, t, c, k).start()

    def side_by_side(ref, t, c, count):
        return jnp.concatenate([ref[t, c, j] for j in range(count)], axis=1)

    def dot(inputs, first, end, first_out, end_out):
        return jnp.dot(
            inputs,
            dense[first * bs : end * bs, first_out * bs : end_out * bs],
            preferred_element_type=jnp.float32,
        )

    def own_term(t, c):
        terms = side_by_side(trace, 0, c, nb).astype(jnp.float32)
        own_sum[c] = terms + dot(side_by_side(trace, t, c, nb), 0, nb, 0, nb)

    for c in range(CHUNKS):
        loads[c].wait()
        for j in (*range(nb - FX, nb), *range(nb - FX)):
            trace[0, c, j] = raw[c, j].astype(jnp.float32).T.astype(trace.dtype)
            if j == FX - 1:
                if c == 0:
                    pl.semaphore_wait(barrier, greeted)
                remote(0, c, 0).start()
                remote(0, c, 1).start()
        send_edges(0, c)
    ops_load.start()

    table_copy.wait()
    ops_load.wait()
    merged[slots] = jnp.zeros((bs, bs), merged.dtype)

    def merge(p, total):
        total = jnp.where(places[1, p] > 0, total, 0.0) + ops[places[0, p]].astype(jnp.float32)
        merged[p] = total.T.astype(merged.dtype)
        return total

    lax.fori_loop(0, slots, merge, jnp.zeros((bs, bs), jnp.float32), unroll=4)
    for i in range(ni):
        for j in range(nb):
            cell = i * STRIDE + j
            dense[i * bs : (i + 1) * bs, j * bs : (j + 1) * bs] = merged[
                places[2 + cell // LANES, cell % LANES]
            ]
    for c in range(CHUNKS):
        forward(0, c)
    for c in range(CHUNKS):
        own_term(0, c)

    for t in range(ITERS):
        for c in range(CHUNKS):
            @pl.when(plain_below)
            def _():
                remote(t, c, 2).wait_recv()

            @pl.when(plain_above)
            def _():
                remote(t, c, 3).wait_recv()

            for way in ways:
                @pl.when(way[1])
                def _():
                    for k in range(EMAX):
                        onward(way, t, c, k).wait_recv()

            own_sum[c] += dot(
                side_by_side(edges_in, t, c, 2 * EMAX), nb + 2 * FX, ni, 0, nb
            )
            remote(t, c, 0).wait_recv()
            remote(t, c, 1).wait_recv()

            faces = side_by_side(faces_in, t, c, 2 * FX)

            def finish(first, end):
                total = own_sum[c, :, first * bs : end * bs] + dot(
                    faces, nb, nb + 2 * FX, first, end
                )
                if t == ITERS - 1:
                    result[:, c * width : (c + 1) * width] = total.T.astype(result.dtype)
                else:
                    for j in range(first, end):
                        trace[t + 1, c, j] = total[:, (j - first) * bs : (j - first + 1) * bs].astype(
                            trace.dtype
                        )

            if t == ITERS - 1:
                finish(0, nb)
                if c == 0:
                    forward(t, 1)
            else:
                finish(nb - FX, nb)
                remote(t + 1, c, 0).start()
                finish(0, FX)
                remote(t + 1, c, 1).start()
                finish(FX, nb - FX)
                send_edges(t + 1, c)
                if c == 1:
                    forward(t + 1, 0)
                elif t > 0:
                    forward(t, 1)
                own_term(t + 1, c)

    for t in range(ITERS):
        for c in range(CHUNKS):
            remote(t, c, 0).wait_send()
            remote(t, c, 1).wait_send()

            @pl.when(plain_above)
            def _():
                remote(t, c, 2).wait_send()

            @pl.when(plain_below)
            def _():
                remote(t, c, 3).wait_send()

            for way in ways:
                @pl.when(way[0])
                def _():
                    for k in range(EMAX):
                        crossing(way, t, c, k).wait_send()

                for k in range(EMAX):
                    if (c, k) in RELAYS:
                        @pl.when(gy == way[5](RELAYS[c, k]))
                        def _():
                            onward(way, t, c, k).wait_send()


def shards(sizes, source, op_blocks, op_in, op_out, op_count, edge_up, edge_down):
    rows, columns = source.shape[2:]
    bs = op_blocks.shape[3]
    slots = op_in.shape[2]
    nb = rows // bs
    ni = nb + 2 * FX + 2 * EMAX
    width = columns // CHUNKS
    bf16 = jnp.bfloat16
    in_smem = pl.BlockSpec(memory_space=pltpu.SMEM)
    in_vmem = pl.BlockSpec(memory_space=pltpu.VMEM)
    anywhere = pl.BlockSpec(memory_space=pl.ANY)
    out = pl.pallas_call(
        functools.partial(sweep_kernel, sizes),
        out_shape=pltpu.VMEM((rows, columns), bf16),
        in_specs=[anywhere] * 4 + [in_smem] + [anywhere] * 2,
        out_specs=in_vmem,
        scratch_shapes=[
            pltpu.VMEM((CHUNKS, nb, bs, width), bf16),
            pltpu.VMEM((ITERS, CHUNKS, nb, width, bs), bf16),
            pltpu.VMEM((ITERS, CHUNKS, EMAX, width, bs), bf16),
            pltpu.VMEM((ITERS, CHUNKS, 2 * FX, width, bs), bf16),
            pltpu.VMEM((ITERS, CHUNKS, 2 * EMAX, width, bs), bf16),
            pltpu.VMEM((ITERS, CHUNKS, EMAX, width, bs), bf16),
            pltpu.VMEM((ITERS, CHUNKS, EMAX, width, bs), bf16),
            pltpu.VMEM((CHUNKS, width, rows), jnp.float32),
            pltpu.VMEM((slots, bs, bs), bf16),
            pltpu.VMEM((slots + 1, bs, bs), bf16),
            pltpu.VMEM((ni * bs, rows), bf16),
            pltpu.VMEM((1, slots), jnp.int32),
            pltpu.VMEM((1, slots), jnp.int32),
            pltpu.VMEM((1, LANES), jnp.int32),
            pltpu.VMEM((1, LANES), jnp.int32),
            pltpu.VMEM((8, LANES), jnp.int32),
            pltpu.SMEM((8, LANES), jnp.int32),
            pltpu.SMEM((1, EMAX), jnp.int32),
            pltpu.SMEM((1, EMAX), jnp.int32),
            pltpu.SemaphoreType.DMA((CHUNKS + 1,)),
            pltpu.SemaphoreType.DMA((4,)),
            pltpu.SemaphoreType.DMA,
            pltpu.SemaphoreType.DMA((ITERS, CHUNKS, 4)),
            pltpu.SemaphoreType.DMA((ITERS, CHUNKS, 4)),
            pltpu.SemaphoreType.DMA((ITERS, CHUNKS, EMAX)),
            pltpu.SemaphoreType.DMA((ITERS, CHUNKS, EMAX)),
            pltpu.SemaphoreType.DMA((ITERS, CHUNKS, EMAX)),
            pltpu.SemaphoreType.DMA((ITERS, CHUNKS, EMAX)),
        ],
        compiler_params=pltpu.CompilerParams(
            collective_id=0, has_side_effects=True, vmem_limit_bytes=VMEM_LIMIT
        ),
    )(
        source.reshape(nb, bs, columns),
        op_blocks.reshape(slots, bs, bs),
        op_in.reshape(1, slots),
        op_out.reshape(1, slots),
        op_count,
        edge_up.reshape(1, EMAX),
        edge_down.reshape(1, EMAX),
    )
    return out.reshape(source.shape)


def solution(mesh):
    placed = (
        P("gx", "gy", None, None),
        P("gx", "gy", None, None),
        P("gx", "gy", None),
        P("gx", "gy", None),
        P("gx", "gy"),
        P("gx", "gy", None),
        P("gx", "gy", None),
    )
    sizes = (mesh.shape["gx"], mesh.shape["gy"])
    return jax.shard_map(
        functools.partial(shards, sizes),
        mesh=mesh,
        in_specs=placed,
        out_specs=P("gx", "gy", None, None),
        check_vma=False,
    )
```

```python
import functools

import jax
import jax.numpy as jnp
from jax import lax
from jax.experimental import pallas as pl
from jax.experimental.pallas import tpu as pltpu
from jax.sharding import PartitionSpec as P

FX = 2
EMAX = 2
ITERS = 4
CHUNKS = 2
VMEM_LIMIT = 58 * 1024 * 1024
RELAYS = {(0, 1): 0, (1, 1): 0}
MESH = pl.DeviceIdType.MESH


LANES = 128
STRIDE = 32


def slot_table(in_row, out_row, count, table, slots, nb, ni):
    lanes = lax.broadcasted_iota(jnp.int32, (LANES, LANES), 1)
    subs = lax.broadcasted_iota(jnp.int32, (LANES, LANES), 0)
    row_ids = lax.broadcasted_iota(jnp.int32, (1, LANES), 1)
    is_own = (in_row >= FX) & (in_row < FX + nb)
    place = jnp.where(in_row < FX, in_row + nb, jnp.where(is_own, in_row - FX, in_row))
    cell_row = jnp.where(row_ids < count, place * STRIDE + out_row, 1 << 20)
    cells_t = jnp.broadcast_to(cell_row, (LANES, LANES))
    cells_s = jnp.broadcast_to(
        jnp.sum(jnp.where(lanes == subs, cells_t, 0), axis=1, keepdims=True), (LANES, LANES)
    )
    before = (cells_t < cells_s) | ((cells_t == cells_s) & (lanes < subs))
    rank = jnp.broadcast_to(
        jnp.sum(jnp.where(before, 1, 0), axis=1, keepdims=True), (LANES, LANES)
    )
    perm = jnp.sum(jnp.where(rank == lanes, subs, 0), axis=0, keepdims=True)
    here = jnp.sum(jnp.where(rank == lanes, cells_s, 0), axis=0, keepdims=True)
    previous = jnp.sum(jnp.where(rank + 1 == lanes, cells_s, 0), axis=0, keepdims=True)
    table[0:1, :] = jnp.minimum(perm, slots - 1)
    table[1:2, :] = jnp.where((row_ids > 0) & (here == previous), 1, 0)
    for part in range(-(-ni * STRIDE // LANES)):
        wanted = lanes + part * LANES
        upto = jnp.sum(jnp.where(cells_s <= wanted, 1, 0), axis=0, keepdims=True)
        equal = jnp.sum(jnp.where(cells_s == wanted, 1, 0), axis=0, keepdims=True)
        table[2 + part : 3 + part, :] = jnp.where(equal > 0, upto - 1, slots)


def sweep_kernel(
    sizes, source, blocks, ops_in, ops_out, count, ups_in, downs_in, result,
    raw, trace, relay_in, faces_in, edges_in, up_pick, down_pick, own_sum,
    ops, merged, dense, in_list, out_list, in_row, out_row, table, places, ups, downs,
    load_sem, small_sem, table_sem, send_sem, recv_sem,
    cross_send, cross_recv, relay_send, relay_recv,
):
    n_gx, n_gy = sizes
    nb, width, bs = trace.shape[2:]
    slots, ni = blocks.shape[0], dense.shape[0] // bs
    gx, gy = lax.axis_index("gx"), lax.axis_index("gy")
    right = (lax.rem(gx + 1, n_gx), gy)
    left = (lax.rem(gx + n_gx - 1, n_gx), gy)
    above = (gx, lax.rem(gy + 1, n_gy))
    below = (gx, lax.rem(gy + n_gy - 1, n_gy))
    has_above, has_below = gy < n_gy - 1, gy > 0

    middle = n_gy // 2
    low, high = gy == middle - 1, gy == middle
    up_relays = sorted(set(RELAYS.values()))
    down_relays = [n_gy - 1 - relay for relay in up_relays]
    is_relay = functools.reduce(jnp.logical_or, [gy == r for r in up_relays + down_relays])
    greeted = (
        2
        + has_above.astype(jnp.int32)
        + has_below.astype(jnp.int32)
        + 2 * is_relay.astype(jnp.int32)
        + 2 * len(up_relays) * jnp.logical_or(low, high).astype(jnp.int32)
    )

    barrier = pltpu.get_barrier_semaphore()
    for place in (right, left):
        pl.semaphore_signal(barrier, inc=1, device_id=place, device_id_type=MESH)

    @pl.when(has_above)
    def _():
        pl.semaphore_signal(barrier, inc=1, device_id=above, device_id_type=MESH)

    @pl.when(has_below)
    def _():
        pl.semaphore_signal(barrier, inc=1, device_id=below, device_id_type=MESH)

    @pl.when(is_relay)
    def _():
        for end in (middle - 1, middle):
            pl.semaphore_signal(barrier, inc=1, device_id=(gx, end), device_id_type=MESH)

    @pl.when(jnp.logical_or(low, high))
    def _():
        for relay in up_relays + down_relays:
            pl.semaphore_signal(barrier, inc=1, device_id=(gx, relay), device_id_type=MESH)

    loads = [
        pltpu.make_async_copy(
            source.at[:, :, pl.ds(c * width, width)], raw.at[c], load_sem.at[c]
        )
        for c in range(CHUNKS)
    ]
    ops_load = pltpu.make_async_copy(blocks, ops, load_sem.at[CHUNKS])
    pairs = ((ops_in, in_list), (ops_out, out_list), (ups_in, ups), (downs_in, downs))
    small = [
        pltpu.make_async_copy(src, dst, small_sem.at[k]) for k, (src, dst) in enumerate(pairs)
    ]
    for copy in loads + small:
        copy.start()

    in_row[...] = jnp.zeros_like(in_row)
    out_row[...] = jnp.zeros_like(out_row)
    for copy in small:
        copy.wait()
    in_row[:, 0:slots] = in_list[...]
    out_row[:, 0:slots] = out_list[...]
    slot_table(in_row[...], out_row[...], count[0, 0], table, slots, nb, ni)
    table_copy = pltpu.make_async_copy(table, places, table_sem)
    table_copy.start()

    @pl.when(jnp.logical_not(has_below))
    def _():
        edges_in[:, :, 0:EMAX] = jnp.zeros((ITERS, CHUNKS, EMAX, width, bs), edges_in.dtype)

    @pl.when(jnp.logical_not(has_above))
    def _():
        edges_in[:, :, EMAX:] = jnp.zeros((ITERS, CHUNKS, EMAX, width, bs), edges_in.dtype)

    def remote(t, c, which):
        src, dst, place = (
            (trace.at[t, c, pl.ds(nb - FX, FX)], faces_in.at[t, c, pl.ds(0, FX)], right),
            (trace.at[t, c, pl.ds(0, FX)], faces_in.at[t, c, pl.ds(FX, FX)], left),
            (up_pick.at[t, c], edges_in.at[t, c, pl.ds(0, EMAX)], above),
            (down_pick.at[t, c], edges_in.at[t, c, pl.ds(EMAX, EMAX)], below),
        )[which]
        return pltpu.make_async_remote_copy(
            src_ref=src,
            dst_ref=dst,
            send_sem=send_sem.at[t, c, which],
            recv_sem=recv_sem.at[t, c, which],
            device_id=place,
            device_id_type=MESH,
        )

    ways = (
        (low, high, middle, up_pick, 0, lambda relay: relay),
        (high, low, middle - 1, down_pick, EMAX, lambda relay: n_gy - 1 - relay),
    )

    def crossing(way, t, c, k):
        _, _, end, pick, first, side = way
        relay = side(RELAYS[c, k]) if (c, k) in RELAYS else None
        return pltpu.make_async_remote_copy(
            src_ref=pick.at[t, c, k],
            dst_ref=edges_in.at[t, c, first + k] if relay is None else relay_in.at[t, c, k],
            send_sem=cross_send.at[t, c, k],
            recv_sem=cross_recv.at[t, c, k] if relay is None else relay_recv.at[t, c, k],
            device_id=(gx, end if relay is None else relay),
            device_id_type=MESH,
        )

    def onward(way, t, c, k):
        _, _, end, _, first, _ = way
        return pltpu.make_async_remote_copy(
            src_ref=relay_in.at[t, c, k],
            dst_ref=edges_in.at[t, c, first + k],
            send_sem=relay_send.at[t, c, k],
            recv_sem=cross_recv.at[t, c, k],
            device_id=(gx, end),
            device_id_type=MESH,
        )

    def forward(t, c):
        for (chunk, k), relay in RELAYS.items():
            if chunk == c:
                for way in ways:
                    @pl.when(gy == way[5](relay))
                    def _():
                        crossing(way, t, c, k).wait_recv()
                        onward(way, t, c, k).start()

    plain_above = jnp.logical_and(has_above, jnp.logical_not(low))
    plain_below = jnp.logical_and(has_below, jnp.logical_not(high))

    def send_edges(t, c):
        @pl.when(has_above)
        def _():
            for k in range(EMAX):
                up_pick[t, c, k] = trace[t, c, ups[0, k]]

        @pl.when(has_below)
        def _():
            for k in range(EMAX):
                down_pick[t, c, k] = trace[t, c, downs[0, k]]

        @pl.when(plain_above)
        def _():
            remote(t, c, 2).start()

        @pl.when(plain_below)
        def _():
            remote(t, c, 3).start()

        for way in ways:
            @pl.when(way[0])
            def _():
                for k in range(EMAX):
                    crossing(way, t, c, k).start()

    def side_by_side(ref, t, c, count):
        return jnp.concatenate([ref[t, c, j] for j in range(count)], axis=1)

    def dot(inputs, first, end, first_out, end_out):
        return jnp.dot(
            inputs,
            dense[first * bs : end * bs, first_out * bs : end_out * bs],
            preferred_element_type=jnp.float32,
        )

    def own_term(t, c):
        terms = side_by_side(trace, 0, c, nb).astype(jnp.float32)
        own_sum[c] = terms + dot(side_by_side(trace, t, c, nb), 0, nb, 0, nb)

    for c in range(CHUNKS):
        loads[c].wait()
        for j in (*range(nb - FX, nb), *range(nb - FX)):
            trace[0, c, j] = raw[c, j].astype(jnp.float32).T.astype(trace.dtype)
            if j == FX - 1:
                if c == 0:
                    pl.semaphore_wait(barrier, greeted)
                remote(0, c, 0).start()
                remote(0, c, 1).start()
        send_edges(0, c)
    ops_load.start()

    table_copy.wait()
    ops_load.wait()
    merged[slots] = jnp.zeros((bs, bs), merged.dtype)

    def merge(p, total):
        total = jnp.where(places[1, p] > 0, total, 0.0) + ops[places[0, p]].astype(jnp.float32)
        merged[p] = total.T.astype(merged.dtype)
        return total

    lax.fori_loop(0, slots, merge, jnp.zeros((bs, bs), jnp.float32), unroll=4)
    for c in range(CHUNKS):
        forward(0, c)
    for i in range(ni):
        for j in range(nb):
            cell = i * STRIDE + j
            dense[i * bs : (i + 1) * bs, j * bs : (j + 1) * bs] = merged[
                places[2 + cell // LANES, cell % LANES]
            ]
    for c in range(CHUNKS):
        own_term(0, c)

    for t in range(ITERS):
        for c in range(CHUNKS):
            @pl.when(plain_below)
            def _():
                remote(t, c, 2).wait_recv()

            @pl.when(plain_above)
            def _():
                remote(t, c, 3).wait_recv()

            for way in ways:
                @pl.when(way[1])
                def _():
                    for k in range(EMAX):
                        onward(way, t, c, k).wait_recv()

            own_sum[c] += dot(
                side_by_side(edges_in, t, c, 2 * EMAX), nb + 2 * FX, ni, 0, nb
            )
            remote(t, c, 0).wait_recv()
            remote(t, c, 1).wait_recv()

            faces = side_by_side(faces_in, t, c, 2 * FX)

            def finish(first, end):
                total = own_sum[c, :, first * bs : end * bs] + dot(
                    faces, nb, nb + 2 * FX, first, end
                )
                if t == ITERS - 1:
                    result[:, c * width : (c + 1) * width] = total.T.astype(result.dtype)
                else:
                    for j in range(first, end):
                        trace[t + 1, c, j] = total[:, (j - first) * bs : (j - first + 1) * bs].astype(
                            trace.dtype
                        )

            if t == ITERS - 1:
                finish(0, nb)
            else:
                finish(nb - FX, nb)
                remote(t + 1, c, 0).start()
                finish(0, FX)
                remote(t + 1, c, 1).start()
                finish(FX, nb - FX)
                send_edges(t + 1, c)
                own_term(t + 1, c)
                forward(t + 1, c)

    for t in range(ITERS):
        for c in range(CHUNKS):
            remote(t, c, 0).wait_send()
            remote(t, c, 1).wait_send()

            @pl.when(plain_above)
            def _():
                remote(t, c, 2).wait_send()

            @pl.when(plain_below)
            def _():
                remote(t, c, 3).wait_send()

            for way in ways:
                @pl.when(way[0])
                def _():
                    for k in range(EMAX):
                        crossing(way, t, c, k).wait_send()

                for k in range(EMAX):
                    if (c, k) in RELAYS:
                        @pl.when(gy == way[5](RELAYS[c, k]))
                        def _():
                            onward(way, t, c, k).wait_send()


def shards(sizes, source, op_blocks, op_in, op_out, op_count, edge_up, edge_down):
    rows, columns = source.shape[2:]
    bs = op_blocks.shape[3]
    slots = op_in.shape[2]
    nb = rows // bs
    ni = nb + 2 * FX + 2 * EMAX
    width = columns // CHUNKS
    bf16 = jnp.bfloat16
    in_smem = pl.BlockSpec(memory_space=pltpu.SMEM)
    in_vmem = pl.BlockSpec(memory_space=pltpu.VMEM)
    anywhere = pl.BlockSpec(memory_space=pl.ANY)
    out = pl.pallas_call(
        functools.partial(sweep_kernel, sizes),
        out_shape=pltpu.VMEM((rows, columns), bf16),
        in_specs=[anywhere] * 4 + [in_smem] + [anywhere] * 2,
        out_specs=in_vmem,
        scratch_shapes=[
            pltpu.VMEM((CHUNKS, nb, bs, width), bf16),
            pltpu.VMEM((ITERS, CHUNKS, nb, width, bs), bf16),
            pltpu.VMEM((ITERS, CHUNKS, EMAX, width, bs), bf16),
            pltpu.VMEM((ITERS, CHUNKS, 2 * FX, width, bs), bf16),
            pltpu.VMEM((ITERS, CHUNKS, 2 * EMAX, width, bs), bf16),
            pltpu.VMEM((ITERS, CHUNKS, EMAX, width, bs), bf16),
            pltpu.VMEM((ITERS, CHUNKS, EMAX, width, bs), bf16),
            pltpu.VMEM((CHUNKS, width, rows), jnp.float32),
            pltpu.VMEM((slots, bs, bs), bf16),
            pltpu.VMEM((slots + 1, bs, bs), bf16),
            pltpu.VMEM((ni * bs, rows), bf16),
            pltpu.VMEM((1, slots), jnp.int32),
            pltpu.VMEM((1, slots), jnp.int32),
            pltpu.VMEM((1, LANES), jnp.int32),
            pltpu.VMEM((1, LANES), jnp.int32),
            pltpu.VMEM((8, LANES), jnp.int32),
            pltpu.SMEM((8, LANES), jnp.int32),
            pltpu.SMEM((1, EMAX), jnp.int32),
            pltpu.SMEM((1, EMAX), jnp.int32),
            pltpu.SemaphoreType.DMA((CHUNKS + 1,)),
            pltpu.SemaphoreType.DMA((4,)),
            pltpu.SemaphoreType.DMA,
            pltpu.SemaphoreType.DMA((ITERS, CHUNKS, 4)),
            pltpu.SemaphoreType.DMA((ITERS, CHUNKS, 4)),
            pltpu.SemaphoreType.DMA((ITERS, CHUNKS, EMAX)),
            pltpu.SemaphoreType.DMA((ITERS, CHUNKS, EMAX)),
            pltpu.SemaphoreType.DMA((ITERS, CHUNKS, EMAX)),
            pltpu.SemaphoreType.DMA((ITERS, CHUNKS, EMAX)),
        ],
        compiler_params=pltpu.CompilerParams(
            collective_id=0, has_side_effects=True, vmem_limit_bytes=VMEM_LIMIT
        ),
    )(
        source.reshape(nb, bs, columns),
        op_blocks.reshape(slots, bs, bs),
        op_in.reshape(1, slots),
        op_out.reshape(1, slots),
        op_count,
        edge_up.reshape(1, EMAX),
        edge_down.reshape(1, EMAX),
    )
    return out.reshape(source.shape)


def solution(mesh):
    placed = (
        P("gx", "gy", None, None),
        P("gx", "gy", None, None),
        P("gx", "gy", None),
        P("gx", "gy", None),
        P("gx", "gy"),
        P("gx", "gy", None),
        P("gx", "gy", None),
    )
    sizes = (mesh.shape["gx"], mesh.shape["gy"])
    return jax.shard_map(
        functools.partial(shards, sizes),
        mesh=mesh,
        in_specs=placed,
        out_specs=P("gx", "gy", None, None),
        check_vma=False,
    )
```

```python
import functools

import jax
import jax.numpy as jnp
from jax import lax
from jax.experimental import pallas as pl
from jax.experimental.pallas import tpu as pltpu
from jax.sharding import PartitionSpec as P

FX = 2
EMAX = 2
ITERS = 4
CHUNKS = 2
VMEM_LIMIT = 58 * 1024 * 1024
MESH = pl.DeviceIdType.MESH


LANES = 128
STRIDE = 32


def slot_table(in_row, out_row, count, table, slots, nb, ni):
    lanes = lax.broadcasted_iota(jnp.int32, (LANES, LANES), 1)
    subs = lax.broadcasted_iota(jnp.int32, (LANES, LANES), 0)
    row_ids = lax.broadcasted_iota(jnp.int32, (1, LANES), 1)
    is_own = (in_row >= FX) & (in_row < FX + nb)
    place = jnp.where(in_row < FX, in_row + nb, jnp.where(is_own, in_row - FX, in_row))
    cell_row = jnp.where(row_ids < count, place * STRIDE + out_row, 1 << 20)
    cells_t = jnp.broadcast_to(cell_row, (LANES, LANES))
    cells_s = jnp.broadcast_to(
        jnp.sum(jnp.where(lanes == subs, cells_t, 0), axis=1, keepdims=True), (LANES, LANES)
    )
    before = (cells_t < cells_s) | ((cells_t == cells_s) & (lanes < subs))
    rank = jnp.broadcast_to(
        jnp.sum(jnp.where(before, 1, 0), axis=1, keepdims=True), (LANES, LANES)
    )
    perm = jnp.sum(jnp.where(rank == lanes, subs, 0), axis=0, keepdims=True)
    here = jnp.sum(jnp.where(rank == lanes, cells_s, 0), axis=0, keepdims=True)
    previous = jnp.sum(jnp.where(rank + 1 == lanes, cells_s, 0), axis=0, keepdims=True)
    table[0:1, :] = jnp.minimum(perm, slots - 1)
    table[1:2, :] = jnp.where((row_ids > 0) & (here == previous), 1, 0)
    for part in range(-(-ni * STRIDE // LANES)):
        wanted = lanes + part * LANES
        upto = jnp.sum(jnp.where(cells_s <= wanted, 1, 0), axis=0, keepdims=True)
        equal = jnp.sum(jnp.where(cells_s == wanted, 1, 0), axis=0, keepdims=True)
        table[2 + part : 3 + part, :] = jnp.where(equal > 0, upto - 1, slots)


def sweep_kernel(
    sizes, source, blocks, ops_in, ops_out, count, ups_in, downs_in, result,
    raw, trace, landed, up_pick, down_pick, own_sum,
    ops, merged, dense, in_list, out_list, in_row, out_row, table, places, ups, downs,
    load_sem, small_sem, table_sem, send_sem, recv_sem,
):
    n_gx, n_gy = sizes
    nb, width, bs = trace.shape[2:]
    slots, ni = blocks.shape[0], dense.shape[0] // bs
    gx, gy = lax.axis_index("gx"), lax.axis_index("gy")
    right = (lax.rem(gx + 1, n_gx), gy)
    left = (lax.rem(gx + n_gx - 1, n_gx), gy)
    above = (gx, lax.rem(gy + 1, n_gy))
    below = (gx, lax.rem(gy + n_gy - 1, n_gy))
    has_above, has_below = gy < n_gy - 1, gy > 0

    barrier = pltpu.get_barrier_semaphore()
    for place in (right, left):
        pl.semaphore_signal(barrier, inc=1, device_id=place, device_id_type=MESH)

    @pl.when(has_above)
    def _():
        pl.semaphore_signal(barrier, inc=1, device_id=above, device_id_type=MESH)

    @pl.when(has_below)
    def _():
        pl.semaphore_signal(barrier, inc=1, device_id=below, device_id_type=MESH)

    loads = [
        pltpu.make_async_copy(
            source.at[:, :, pl.ds(c * width, width)], raw.at[c], load_sem.at[c]
        )
        for c in range(CHUNKS)
    ]
    ops_load = pltpu.make_async_copy(blocks, ops, load_sem.at[CHUNKS])
    pairs = ((ops_in, in_list), (ops_out, out_list), (ups_in, ups), (downs_in, downs))
    small = [
        pltpu.make_async_copy(src, dst, small_sem.at[k]) for k, (src, dst) in enumerate(pairs)
    ]
    for copy in loads + small:
        copy.start()

    in_row[...] = jnp.zeros_like(in_row)
    out_row[...] = jnp.zeros_like(out_row)
    for copy in small:
        copy.wait()
    in_row[:, 0:slots] = in_list[...]
    out_row[:, 0:slots] = out_list[...]
    slot_table(in_row[...], out_row[...], count[0, 0], table, slots, nb, ni)
    table_copy = pltpu.make_async_copy(table, places, table_sem)
    table_copy.start()

    @pl.when(jnp.logical_not(has_below))
    def _():
        landed[:, :, 2 * FX : 2 * FX + EMAX] = jnp.zeros((ITERS, CHUNKS, EMAX, width, bs), landed.dtype)

    @pl.when(jnp.logical_not(has_above))
    def _():
        landed[:, :, 2 * FX + EMAX :] = jnp.zeros((ITERS, CHUNKS, EMAX, width, bs), landed.dtype)

    def remote(t, c, which):
        src, dst, place = (
            (trace.at[t, c, pl.ds(nb - FX, FX)], landed.at[t, c, pl.ds(0, FX)], right),
            (trace.at[t, c, pl.ds(0, FX)], landed.at[t, c, pl.ds(FX, FX)], left),
            (up_pick.at[t, c], landed.at[t, c, pl.ds(2 * FX, EMAX)], above),
            (down_pick.at[t, c], landed.at[t, c, pl.ds(2 * FX + EMAX, EMAX)], below),
        )[which]
        return pltpu.make_async_remote_copy(
            src_ref=src,
            dst_ref=dst,
            send_sem=send_sem.at[t, c, which],
            recv_sem=recv_sem.at[t, c, which],
            device_id=place,
            device_id_type=MESH,
        )

    def send_edges(t, c):
        @pl.when(has_above)
        def _():
            for k in range(EMAX):
                up_pick[t, c, k] = trace[t, c, ups[0, k]]
            remote(t, c, 2).start()

        @pl.when(has_below)
        def _():
            for k in range(EMAX):
                down_pick[t, c, k] = trace[t, c, downs[0, k]]
            remote(t, c, 3).start()

    def side_by_side(ref, t, c, first, count):
        return jnp.concatenate([ref[t, c, first + j] for j in range(count)], axis=1)

    def dot(inputs, first, count, first_out, end_out):
        return jnp.dot(
            inputs,
            dense[pl.ds(pl.multiple_of(first * bs, bs), count * bs), first_out * bs : end_out * bs],
            preferred_element_type=jnp.float32,
        )

    crosses = jnp.logical_or(gy == n_gy // 2 - 1, gy == n_gy // 2)
    sooner = jnp.where(crosses, 0, 2 * FX)
    later = 2 * FX - sooner

    def wait_edges(t, c, now):
        @pl.when(jnp.logical_and(now, has_below))
        def _():
            remote(t, c, 2).wait_recv()

        @pl.when(jnp.logical_and(now, has_above))
        def _():
            remote(t, c, 3).wait_recv()

    def wait_faces(t, c, now):
        @pl.when(now)
        def _():
            remote(t, c, 0).wait_recv()
            remote(t, c, 1).wait_recv()

    def own_term(t, c):
        terms = side_by_side(trace, 0, c, 0, nb).astype(jnp.float32)
        own_sum[c] = terms + dot(side_by_side(trace, t, c, 0, nb), 0, nb, 0, nb)

    for c in range(CHUNKS):
        loads[c].wait()
        for j in (*range(nb - FX, nb), *range(nb - FX)):
            trace[0, c, j] = raw[c, j].astype(jnp.float32).T.astype(trace.dtype)
            if j == FX - 1:
                if c == 0:
                    pl.semaphore_wait(
                        barrier, 2 + has_above.astype(jnp.int32) + has_below.astype(jnp.int32)
                    )
                remote(0, c, 0).start()
                remote(0, c, 1).start()
        send_edges(0, c)
    ops_load.start()

    table_copy.wait()
    ops_load.wait()
    merged[slots] = jnp.zeros((bs, bs), merged.dtype)

    def merge(p, total):
        total = jnp.where(places[1, p] > 0, total, 0.0) + ops[places[0, p]].astype(jnp.float32)
        merged[p] = total.T.astype(merged.dtype)
        return total

    lax.fori_loop(0, slots, merge, jnp.zeros((bs, bs), jnp.float32), unroll=4)
    for i in range(ni):
        for j in range(nb):
            cell = i * STRIDE + j
            dense[i * bs : (i + 1) * bs, j * bs : (j + 1) * bs] = merged[
                places[2 + cell // LANES, cell % LANES]
            ]
    for c in range(CHUNKS):
        own_term(0, c)

    for t in range(ITERS):
        for c in range(CHUNKS):
            wait_edges(t, c, jnp.logical_not(crosses))
            wait_faces(t, c, crosses)
            own_sum[c] += dot(
                side_by_side(landed, t, c, sooner, 2 * FX), nb + sooner, 2 * FX, 0, nb
            )
            wait_faces(t, c, jnp.logical_not(crosses))
            wait_edges(t, c, crosses)
            inputs = side_by_side(landed, t, c, later, 2 * FX)

            def finish(first, end):
                total = own_sum[c, :, first * bs : end * bs] + dot(
                    inputs, nb + later, 2 * FX, first, end
                )
                if t == ITERS - 1:
                    result[:, c * width : (c + 1) * width] = total.T.astype(result.dtype)
                else:
                    for j in range(first, end):
                        trace[t + 1, c, j] = total[:, (j - first) * bs : (j - first + 1) * bs].astype(
                            trace.dtype
                        )

            if t == ITERS - 1:
                finish(0, nb)
            else:
                finish(nb - FX, nb)
                remote(t + 1, c, 0).start()
                finish(0, FX)
                remote(t + 1, c, 1).start()
                finish(FX, nb - FX)
                send_edges(t + 1, c)
                own_term(t + 1, c)

    for t in range(ITERS):
        for c in range(CHUNKS):
            remote(t, c, 0).wait_send()
            remote(t, c, 1).wait_send()

            @pl.when(has_above)
            def _():
                remote(t, c, 2).wait_send()

            @pl.when(has_below)
            def _():
                remote(t, c, 3).wait_send()


def shards(sizes, source, op_blocks, op_in, op_out, op_count, edge_up, edge_down):
    rows, columns = source.shape[2:]
    bs = op_blocks.shape[3]
    slots = op_in.shape[2]
    nb = rows // bs
    ni = nb + 2 * FX + 2 * EMAX
    width = columns // CHUNKS
    bf16 = jnp.bfloat16
    in_smem = pl.BlockSpec(memory_space=pltpu.SMEM)
    in_vmem = pl.BlockSpec(memory_space=pltpu.VMEM)
    anywhere = pl.BlockSpec(memory_space=pl.ANY)
    out = pl.pallas_call(
        functools.partial(sweep_kernel, sizes),
        out_shape=pltpu.VMEM((rows, columns), bf16),
        in_specs=[anywhere] * 4 + [in_smem] + [anywhere] * 2,
        out_specs=in_vmem,
        scratch_shapes=[
            pltpu.VMEM((CHUNKS, nb, bs, width), bf16),
            pltpu.VMEM((ITERS, CHUNKS, nb, width, bs), bf16),
            pltpu.VMEM((ITERS, CHUNKS, 2 * FX + 2 * EMAX, width, bs), bf16),
            pltpu.VMEM((ITERS, CHUNKS, EMAX, width, bs), bf16),
            pltpu.VMEM((ITERS, CHUNKS, EMAX, width, bs), bf16),
            pltpu.VMEM((CHUNKS, width, rows), jnp.float32),
            pltpu.VMEM((slots, bs, bs), bf16),
            pltpu.VMEM((slots + 1, bs, bs), bf16),
            pltpu.VMEM((ni * bs, rows), bf16),
            pltpu.VMEM((1, slots), jnp.int32),
            pltpu.VMEM((1, slots), jnp.int32),
            pltpu.VMEM((1, LANES), jnp.int32),
            pltpu.VMEM((1, LANES), jnp.int32),
            pltpu.VMEM((8, LANES), jnp.int32),
            pltpu.SMEM((8, LANES), jnp.int32),
            pltpu.SMEM((1, EMAX), jnp.int32),
            pltpu.SMEM((1, EMAX), jnp.int32),
            pltpu.SemaphoreType.DMA((CHUNKS + 1,)),
            pltpu.SemaphoreType.DMA((4,)),
            pltpu.SemaphoreType.DMA,
            pltpu.SemaphoreType.DMA((ITERS, CHUNKS, 4)),
            pltpu.SemaphoreType.DMA((ITERS, CHUNKS, 4)),
        ],
        compiler_params=pltpu.CompilerParams(
            collective_id=0, has_side_effects=True, vmem_limit_bytes=VMEM_LIMIT
        ),
    )(
        source.reshape(nb, bs, columns),
        op_blocks.reshape(slots, bs, bs),
        op_in.reshape(1, slots),
        op_out.reshape(1, slots),
        op_count,
        edge_up.reshape(1, EMAX),
        edge_down.reshape(1, EMAX),
    )
    return out.reshape(source.shape)


def solution(mesh):
    placed = (
        P("gx", "gy", None, None),
        P("gx", "gy", None, None),
        P("gx", "gy", None),
        P("gx", "gy", None),
        P("gx", "gy"),
        P("gx", "gy", None),
        P("gx", "gy", None),
    )
    sizes = (mesh.shape["gx"], mesh.shape["gy"])
    return jax.shard_map(
        functools.partial(shards, sizes),
        mesh=mesh,
        in_specs=placed,
        out_specs=P("gx", "gy", None, None),
        check_vma=False,
    )
```
